32 devices in a mesh: freq: 1, tile: 32 (over z, y, x, core).
Axes of the slice: x: 2, y: 2, z: 4, core: 2. Of those that a mesh axis runs over, the one named last changes fastest.
Arguments:
- voltages: bfloat16 [4, 4096, 2, 2048], P(None, ('freq', 'tile')), may hold values from -4 to 4
- scales: int32 [4, 4096, 8], P(None, ('freq', 'tile')), may hold values from 1 to 3
- owner_half: int32 [4, 8], replicated, may hold values from 0 to 1, as said below
Outputs:
- visibilities: float32 [1, 32, 5, 512, 1024], P(None, ('freq', 'tile'))
The draws below stay inside these ranges and needn't reach their ends.
Inputs may be any that keep to these rules, and one draw needn't show every extreme that they name: owner_half[c, b] + owner_half[c, (b + 4) mod 8] = 1 for every channel c and block b.
All inputs are finite; a program needn't handle non-finite values.
Results may differ from the reference program's by a relative error of at most 0.0026.
Values may be sent and summed in bfloat16 or wider, within the bound.
No kernel may reach another device: no remote copies, remote signals or barrier semaphores. Data moves between devices by JAX's collectives and lax.ppermute only.
A program may use at most 192 MiB of HBM per device.

```python
import jax
import jax.numpy as jnp
from jax import lax

NI = 4096
INPUTS_PER_BLOCK = 512
CHANNELS_PER_BIN = 4
SAMPLES = 2048
SBLK = 256
CHANNELS = 4
NB = 8
DISTANCE_SLOTS = 5
SCALES = 8
N_FREQ = 1
N_TILE = 32


def draw_owner_half(key, part):
    key = jax.random.fold_in(key, 7)
    first_half = jax.random.randint(key, (CHANNELS, NB // 2), 0, 2).astype(jnp.int32)
    return jnp.concatenate([first_half, 1 - first_half], axis=1).astype(jnp.int32)


def place_ends(drawn, own_key, least, top_value):
    longest = drawn.shape.index(max(drawn.shape))
    spots = []
    for shift in (0, 1):
        where = [jax.random.randint(jax.random.fold_in(own_key, axis), (), 0, length) for axis, length in enumerate(drawn.shape)]
        where[longest] = (where[longest] + shift) % drawn.shape[longest]
        spots.append(tuple(where))
    return drawn.at[spots[0]].set(least).at[spots[1]].set(top_value)


def level_of(rng, dims, cuts, smallest, top_value):
    def one(dim, shards_of):
        draws = jax.random.uniform(jax.random.fold_in(jax.random.fold_in(rng, 6), dim), (shards_of,), jnp.float32, smallest / len(cuts), top_value / len(cuts))
        return jnp.repeat(jnp.exp(draws), dims[dim] // shards_of).reshape((-1,) + (1,) * (len(dims) - dim - 1))

    factor_of = one(*cuts[0])
    for cut in cuts[1:]:
        factor_of = factor_of * one(*cut)
    return factor_of


def noise(stream_key, extent, scale, reach, cuts=(), dtype=jnp.bfloat16):
    drawn = scale * jax.random.normal(stream_key, extent, jnp.float32)
    if cuts:
        drawn = drawn * level_of(stream_key, extent, cuts, -0.22, 0.18)
    return jnp.clip(drawn, -reach, reach).astype(dtype)


def setup_inputs(seed: int = 0) -> dict:
    key_list = jax.random.split(jax.random.key(seed), 4)
    voltages = noise(key_list[0], (CHANNELS, NI, 2, SAMPLES), 0.5, 4.0, ((1, 32),))
    scales = place_ends(jax.random.randint(key_list[1], (CHANNELS, NI, SCALES), 1, 4), jax.random.fold_in(key_list[1], 1), 1, 3).astype(jnp.int32)
    owner_half = draw_owner_half(jax.random.fold_in(key_list[3], 71), 0)
    return dict(voltages=voltages, scales=scales, owner_half=owner_half)


def reference(voltages, scales, owner_half):
    channels = voltages.shape[0]
    time_len = voltages.shape[3]
    group_count = scales.shape[2]
    shaped = voltages.astype(jnp.float32).reshape(channels, NI, 2, group_count, SBLK)
    factor = scales.astype(jnp.float32)[:, :, None, :, None]
    samples_x = (shaped * factor).astype(jnp.bfloat16).reshape(channels, NI, 2, time_len)
    blocks = samples_x.reshape(channels, INPUTS_PER_BLOCK, NB, 2, time_len).transpose(0, 2, 1, 3, 4)
    half_span = NB // 2
    inverse_map = 1.0 / SAMPLES

    def one_channel(channel_item):
        chan_blocks, own_row = channel_item
        col_blk = chan_blocks.astype(jnp.float32)
        swapped = jnp.stack([col_blk[:, :, 1], -col_blk[:, :, 0]], axis=2)
        right_blk = jnp.concatenate([col_blk, swapped], axis=1)
        tiles = []
        for distance in range(half_span + 1):
            rows_blk = jnp.roll(col_blk, distance, axis=0)
            tile_val = jnp.einsum("bmkt,bnkt->bmn", rows_blk, right_blk) * inverse_map
            if distance == half_span:
                tile_val = jnp.where(own_row[:, None, None] == 1, tile_val, jnp.zeros_like(tile_val))
            tiles.append(tile_val)
        return jnp.stack(tiles, axis=1)

    output_tiles = lax.map(one_channel, (blocks, owner_half))
    step_width = N_TILE // CHANNELS_PER_BIN
    baseline_count = NB // step_width
    output_tiles = output_tiles.reshape(N_FREQ, CHANNELS_PER_BIN, baseline_count, step_width, DISTANCE_SLOTS, INPUTS_PER_BLOCK, 2 * INPUTS_PER_BLOCK)
    output_tiles = output_tiles.transpose(2, 0, 3, 1, 4, 5, 6)
    return output_tiles.reshape(baseline_count, N_FREQ * N_TILE, DISTANCE_SLOTS, INPUTS_PER_BLOCK, 2 * INPUTS_PER_BLOCK)
```

```python
import functools

import jax
import jax.numpy as jnp
from jax import lax
from jax.experimental import pallas as pl
from jax.experimental.pallas import tpu as pltpu
from jax.sharding import PartitionSpec as P

CHANNELS_PER_BIN = 4
NB = 8
LINES = 2
DEPTH = NB // LINES
HALF = NB // 2
UP = (2, 3, 4, 5, 6, 7)
DOWN = (4, 5, 6, 7, 0, 1)
SHORT_UP = (0, 1)
SHORT_DOWN = (2, 3)
PARTS = 4
EXCHANGES = ((0, 1), (1, 4))
STEPS = ((0, 0), (0, 1), (1, 0), (0, 2), (1, 1), (2, 0), (1, 2), (3, 0), (2, 1), (3, 1), (2, 2), (3, 2))
GATHERS = {0: (0,), 2: (1,), 4: (2,), 5: (3,)}
TILES = {7: (0,), 9: (1,), 13: (2, 3)}
SIDE = 6
VMEM_BYTES = 56 * 1024 * 1024
STEP_BYTES = 4_000_000

KINDS = range(2 * NB)


def place(kind):
    return kind // 4, kind // 2 % 2, kind % 2


def along(name, kind):
    z, y, parity = place(kind)
    step = 1 if (name == "a") == (parity == 0) else -1
    if 0 <= z + step < DEPTH:
        return 4 * (z + step) + 2 * y + parity, True
    return 4 * z + 2 * y + 1 - parity, False


def upward(parity):
    return "a" if parity == 0 else "b"


def downward(parity):
    return "b" if parity == 0 else "a"


def my_kind(lanes):
    me = lax.axis_index("tile")
    return me // lanes * 2 + me % 2


def needed(u):
    return [(u - s) % NB for s in range(HALF + 1)]


def device_pairs(step, positions, lanes):
    pairs = []
    for g in range(positions):
        kind = step(g // lanes * 2 + g % 2)
        pairs.append((g, kind // 2 * lanes + g % lanes // 2 * 2 + kind % 2))
    return pairs


class Plan:
    def __init__(self):
        self.held = {}

    def own(self, name, part, blocks):
        self.held[name] = [[(part,) + place(k)[:2] + (b,) for b in blocks(place(k)[2])] for k in KINDS]

    def move(self, source, target, step):
        got = [None] * len(KINDS)
        for kind in KINDS:
            goal, useful = step(kind)
            items = self.held[source][kind]
            got[goal] = list(items) if useful else [None] * len(items)
        self.held[target] = got

    def find(self, kind, item, names):
        for name in names:
            if item in self.held[name][kind]:
                return name, self.held[name][kind].index(item)
        return None


def runs(picks):
    out = []
    for dst, name, src in picks:
        if out and out[-1][1] == name and out[-1][0] + out[-1][3] == dst and out[-1][2] + out[-1][3] == src:
            out[-1][3] += 1
        else:
            out.append([dst, name, src, 1])
    return [tuple(r) for r in out]


def copies_kernel(names, after, plan, patched, outs, lanes, *refs):
    ins = dict(zip(names, refs[: len(names)]))
    targets = dict(zip(list(patched) + list(outs), refs[len(names) + 1 + after : -3]))
    through, sems = refs[-2:]
    me = my_kind(lanes)
    for kind, todo in plan.items():

        @pl.when(me == kind)
        def _(todo=todo):
            started, onward, at = [], [], 0
            for i, (target, dst, name, src, length) in enumerate(todo):
                goal = targets[target].at[pl.ds(dst, length)]
                if target in patched:
                    onward.append((i, through.at[pl.ds(at, length)], goal))
                    goal = through.at[pl.ds(at, length)]
                    at += length
                copy = pltpu.make_async_copy(ins[name].at[pl.ds(src, length)], goal, sems.at[0, i])
                copy.start()
                started.append(copy)
            for copy in started:
                copy.wait()
            started = [pltpu.make_async_copy(src, goal, sems.at[1, i]) for i, src, goal in onward]
            for copy in started:
                copy.start()
            for copy in started:
                copy.wait()


def run_copies(arrays, names, after, plan, patched, outs, lanes):
    shape = arrays["a0.0"].shape[1:]
    dtype = arrays["a0.0"].dtype
    any_spec = pl.BlockSpec(memory_space=pl.ANY)
    out_shape = [jax.ShapeDtypeStruct(arrays[n].shape, dtype) for n in patched]
    out_shape += [jax.ShapeDtypeStruct((slots,) + shape, dtype) for slots in outs.values()]
    most = max(1, max(len(todo) for todo in plan.values()))
    token = arrays["token"]
    aliases = {names.index(n): i for i, n in enumerate(patched)}
    aliases[len(names)] = len(out_shape)
    got = pl.pallas_call(
        functools.partial(copies_kernel, names, len(after), plan, patched, list(outs), lanes),
        out_shape=out_shape + [jax.ShapeDtypeStruct(token.shape, token.dtype)],
        in_specs=[any_spec] * (len(names) + 1 + len(after)),
        out_specs=[any_spec] * len(patched) + [pl.BlockSpec(memory_space=pltpu.VMEM)] * len(outs) + [any_spec],
        scratch_shapes=[pltpu.VMEM((4,) + shape, dtype), pltpu.SemaphoreType.DMA((2, most))],
        input_output_aliases=aliases,
        compiler_params=pltpu.CompilerParams(vmem_limit_bytes=VMEM_BYTES),
        cost_estimate=pl.CostEstimate(flops=0, bytes_accessed=STEP_BYTES, transcendentals=0),
        name="pick",
    )(*[arrays[n] for n in names], token, *[arrays[n] for n in after])
    for n, value in zip(list(patched) + list(outs) + ["token"], got):
        arrays[n] = value


def gather_kernel(plan, lanes, start, own, token, a, b, token_out, sems):
    senders, rows = own.shape[0], own.shape[4]
    targets = {"a": a, "b": b}
    me = my_kind(lanes)
    for kind, todo in plan.items():

        @pl.when(me == kind)
        def _(todo=todo):
            started = []
            for lane in range(senders):
                at = pl.ds(lane * rows, rows)
                for i, (target, dst, src, length) in enumerate(todo):
                    copy = pltpu.make_async_copy(
                        own.at[lane, pl.ds(src, length), :, :, :, pl.ds(start, a.shape[-1])],
                        targets[target].at[pl.ds(dst, length), :, :, at],
                        sems.at[lane, i],
                    )
                    copy.start()
                    started.append(copy)
            for copy in started:
                copy.wait()


def run_gather(arrays, part, own, start, samples, plan, lanes):
    senders, _, two, split, rows, _ = own.shape
    shape = (two, split, senders * rows, samples)
    token = arrays["token"]
    any_spec = pl.BlockSpec(memory_space=pl.ANY)
    vmem_spec = pl.BlockSpec(memory_space=pltpu.VMEM)
    most = max(len(todo) for todo in plan.values())
    arrays["a0.%d" % part], arrays["b0.%d" % part], arrays["token"] = pl.pallas_call(
        functools.partial(gather_kernel, plan, lanes, start),
        out_shape=[jax.ShapeDtypeStruct((n,) + shape, own.dtype) for n in (len(UP), len(DOWN))]
        + [jax.ShapeDtypeStruct(token.shape, token.dtype)],
        in_specs=[any_spec] * 2,
        out_specs=[vmem_spec] * 2 + [any_spec],
        scratch_shapes=[pltpu.SemaphoreType.DMA((senders, most))],
        input_output_aliases={1: 2},
        compiler_params=pltpu.CompilerParams(vmem_limit_bytes=VMEM_BYTES),
        cost_estimate=pl.CostEstimate(flops=0, bytes_accessed=0, transcendentals=0),
        name="gather",
    )(own, token)


def tiles_kernel(names, plan, lanes, scale, first, last, *refs):
    ins = dict(zip(names, refs[: len(names)]))
    refs = refs[len(names) :]
    flag = acc = None
    if last:
        flag, refs = refs[0], refs[1:]
    if not first:
        acc, refs = refs[0], refs[1:]
    _, out, _, held, sems = refs
    me = my_kind(lanes)
    s = pl.program_id(0)

    @pl.when(s == 0)
    def _():
        for kind, todo in plan.items():

            @pl.when(me == kind)
            def _(todo=todo):
                for slot, row, name, src in todo:
                    pltpu.make_async_copy(ins[name].at[src], held.at[slot, :, :, row], sems.at[slot, row]).start()

    for row in range(NB):
        pltpu.make_async_copy(held.at[s, :, :, row], held.at[s, :, :, row], sems.at[s, row]).wait()
    rows = held.shape[2] * held.shape[3] * held.shape[4]
    samples = held.shape[5]

    def mul(a, b):
        return lax.dot_general(a, b, (((1,), (1,)), ((), ())), preferred_element_type=jnp.float32)

    ar = held[s, 0].reshape(rows, samples)
    ai = held[s, 1].reshape(rows, samples)
    br = held[0, 0].reshape(rows, samples)
    bi = held[0, 1].reshape(rows, samples)
    real = (mul(ar, br) + mul(ai, bi)) * scale
    imag = (mul(ar, bi) - mul(ai, br)) * scale
    if not first:
        real = real + acc[0, :, :rows]
        imag = imag + acc[0, :, rows:]
    if last:
        keep = jnp.logical_or(s < HALF, flag[0] == 1)
        real = jnp.where(keep, real, 0.0)
        imag = jnp.where(keep, imag, 0.0)
    out[0, :, :rows] = real
    out[0, :, rows:] = imag


def run_tiles(arrays, names, plan, lanes, scale, acc, flag):
    token = arrays["token"]
    shape = arrays[names[0]].shape[1:]
    rows = shape[1] * shape[2] * NB
    samples = shape[3]
    any_spec = pl.BlockSpec(memory_space=pl.ANY)
    tile_spec = pl.BlockSpec((1, rows, 2 * rows), lambda s: (s, 0, 0))
    operands = [arrays[n] for n in names]
    in_specs = [any_spec] * len(names)
    aliases = {}
    if flag is not None:
        operands.append(flag)
        in_specs.append(pl.BlockSpec(memory_space=pltpu.SMEM))
    if acc is not None:
        aliases = {len(operands): 0}
        operands.append(acc)
        in_specs.append(tile_spec)
    aliases[len(operands)] = 1
    operands.append(token)
    in_specs.append(any_spec)
    held = (HALF + 1, 2, shape[1], NB, shape[2], samples)
    result, arrays["token"] = pl.pallas_call(
        functools.partial(tiles_kernel, names, plan, lanes, scale, acc is None, flag is not None),
        grid=(HALF + 1,),
        out_shape=[
            jax.ShapeDtypeStruct((HALF + 1, rows, 2 * rows), jnp.float32),
            jax.ShapeDtypeStruct(token.shape, token.dtype),
        ],
        in_specs=in_specs,
        out_specs=[tile_spec, any_spec],
        scratch_shapes=[pltpu.VMEM(held, jnp.bfloat16), pltpu.SemaphoreType.DMA((HALF + 1, NB))],
        input_output_aliases=aliases,
        compiler_params=pltpu.CompilerParams(vmem_limit_bytes=VMEM_BYTES),
        cost_estimate=pl.CostEstimate(flops=0, bytes_accessed=0, transcendentals=0),
        name="tiles",
    )(*operands)
    return result


def dequantize(voltages, scales):
    groups = scales.shape[-1]
    shaped = voltages.reshape(voltages.shape[:-1] + (groups, voltages.shape[-1] // groups))
    product = shaped.astype(jnp.float32) * scales.astype(jnp.float32)[..., None]
    return product.astype(jnp.bfloat16).reshape(voltages.shape)


def exchange(voltages, scales, freq_count, lanes):
    samples = voltages.shape[3]
    rows = voltages.shape[1] // NB
    split = (freq_count, lanes, rows, NB)
    x = dequantize(voltages.reshape(split + (2, samples)), scales.reshape(split + (1, scales.shape[2])))
    x = x.transpose(1, 3, 4, 0, 2, 5)
    if freq_count > 1:
        x = lax.all_to_all(x, "freq", 3, 3, tiled=True)
    positions = lax.axis_size("tile")
    groups = [list(range(g, g + lanes)) for g in range(0, positions, lanes)]
    x = lax.all_to_all(x, "tile", 0, 0, axis_index_groups=groups, tiled=True)
    if freq_count > 1:
        x = x.transpose(1, 2, 3, 0, 4, 5)
        x = x.reshape((1,) + x.shape[:3] + (lanes * rows, samples))
    return x


class Turn:
    def __init__(self, owns, lanes):
        self.owns, self.lanes = owns, lanes
        self.positions = lax.axis_size("tile")
        self.plan = Plan()
        self.arrays = {"token": jnp.zeros((8, 128), jnp.int32)}
        for part in range(len(owns)):
            self.plan.own("blocks.%d" % part, part, lambda parity: range(NB))
            self.plan.own("a0.%d" % part, part, lambda parity: DOWN if parity else UP)
            self.plan.own("b0.%d" % part, part, lambda parity: UP if parity else DOWN)
        self.sent = [set() for _ in KINDS]
        self.here = []
        self.crossed = []

    def move(self, source, target, step):
        self.plan.move(source, target, step)
        pairs = device_pairs(lambda kind: step(kind)[0], self.positions, self.lanes)
        self.arrays[target] = lax.ppermute(self.arrays[source], "tile", pairs)

    def gather(self, part):
        todo = {}
        for kind in KINDS:
            todo[kind] = []
            for name in "ab":
                blocks = [item[3] for item in self.plan.held["%s0.%d" % (name, part)][kind]]
                for d, _, src, length in runs([(i, "", b) for i, b in enumerate(blocks)]):
                    todo[kind].append((name, d, src, length))
        run_gather(self.arrays, part, *self.owns[part], todo, self.lanes)
        self.here += ["a0.%d" % part, "b0.%d" % part]

    def along(self, part, stage):
        for name in "ab":
            self.move("%s%d.%d" % (name, stage, part), "%s%d.%d" % (name, stage + 1, part), functools.partial(along, name))

    def arrived(self, part, stage):
        names = ["%s%d.%d" % (name, stage, part) for name in "ab"]
        self.here += names
        return names

    def choose(self, kind, most, parts):
        wanted = []
        y = place(kind)[1]
        for part in parts:
            for source in range(DEPTH):
                for b in needed(kind // 2 ^ 1):
                    item = (part, source, y, b)
                    where = self.plan.find(kind, item, self.here)
                    if item not in self.sent[kind] and where and len(wanted) < most:
                        wanted.append((item, where))
        wanted.sort(key=lambda w: w[1])
        self.sent[kind].update(w[0] for w in wanted)
        return wanted

    def prepare(self, part=None, stage=None, side=None, after=(), parts=None):
        todo = {kind: [] for kind in KINDS}
        patched, outs = [], {}
        if part is not None:
            patched = ["%s%d.%d" % (name, stage, part) for name in "ab"]
        if stage:
            for kind in KINDS:
                z, y, parity = place(kind)
                for low, way, blocks in ((z, upward, SHORT_UP), (DEPTH - 1 - z, downward, SHORT_DOWN)):
                    if low == stage - 1:
                        target, dst = "%s%d.%d" % (way(parity), stage, part), 2 * (stage - 1)
                        items = [(part, z, y, b) for b in blocks]
                        found = [self.plan.find(kind, item, ["a0.%d" % part, "b0.%d" % part]) for item in items]
                        for d, name, src, length in runs([(dst + i, n, k) for i, (n, k) in enumerate(found)]):
                            todo[kind].append((target, d, name, src, length))
                        self.plan.held[target][kind][dst : dst + len(items)] = items
        if side is not None:
            name, most = side
            chosen = [self.choose(kind, most, range(len(self.owns)) if parts is None else parts) for kind in KINDS]
            slots = max(len(c) for c in chosen)
            outs = {"side" + name: slots}
            for kind in KINDS:
                self.plan.held.setdefault("side" + name, []).append(
                    [w[0] for w in chosen[kind]] + [None] * (slots - len(chosen[kind]))
                )
                picks = [(i, n, k) for i, (_, (n, k)) in enumerate(chosen[kind])]
                todo[kind] += [("side" + name,) + r for r in runs(picks)]
        used = {t[2] for kind in KINDS for t in todo[kind]}
        names = [n for n in self.here if n in used or n in patched]
        after = [n for n in after if n not in names]
        run_copies(self.arrays, names, after, todo, patched, outs, self.lanes)
        if side is not None:
            self.move("side" + name, "got" + name, lambda kind: (kind ^ 2, True))
            self.crossed.append("got" + name)

    def tiles(self, part, scale, result, flag):
        names = [n for n in self.here if n.endswith(".%d" % part)] + self.crossed
        todo = {}
        for kind in KINDS:
            todo[kind] = []
            for s, b in enumerate(needed(kind // 2)):
                for row in range(NB):
                    where = self.plan.find(kind, (part, row // 2, row % 2, b), names)
                    assert where is not None
                    todo[kind].append((s, row) + where)
        used = {t[2] for kind in KINDS for t in todo[kind]}
        return run_tiles(self.arrays, [n for n in names if n in used], todo, self.lanes, scale, result, flag)


def shards(voltages, scales, owner_half):
    time_len = voltages.shape[3]
    group_len = time_len // scales.shape[2]
    freq_count = lax.axis_size("freq")
    lanes = CHANNELS_PER_BIN
    tile_pos = lax.axis_index("tile")
    chan_idx = lax.axis_index("freq") * lanes + tile_pos % lanes
    flag = lax.dynamic_slice(owner_half, (chan_idx, tile_pos // lanes), (1, 1)).reshape(1)
    samples = time_len // PARTS
    owns = []
    for first, last in EXCHANGES:
        start, stop = first * samples, last * samples
        own = exchange(
            voltages[..., start:stop], scales[..., start // group_len : stop // group_len], freq_count, lanes
        )
        owns += [(own, (part - first) * samples, samples) for part in range(first, last)]
    scale = 1.0 / time_len
    turn = Turn(owns, lanes)
    result = None
    known = 0
    for n, (part, stage) in enumerate(STEPS):
        for fresh in GATHERS.get(n, ()):
            turn.gather(fresh)
        done = []
        while known < n and (known <= n - 2 or STEPS[known][0] == part):
            done += turn.arrived(STEPS[known][0], STEPS[known][1] + 1)
            known += 1
        if n >= 2:
            done = done + ["got%d" % (n - 2)]
        turn.prepare(part, stage, side=(str(n), SIDE), after=done)
        turn.along(part, stage)
        for ready in TILES.get(n, ()):
            result = turn.tiles(ready, scale, result, None)
    for n in (len(STEPS), len(STEPS) + 1):
        done = ["got%d" % (n - 2)]
        while known < n - 1:
            done += turn.arrived(STEPS[known][0], STEPS[known][1] + 1)
            known += 1
        turn.prepare(side=(str(n), SIDE if n == len(STEPS) else 99), after=done)
    for ready in TILES.get(n, ()):
        result = turn.tiles(ready, scale, result, flag if ready == PARTS - 1 else None)
    return result[None, None]


def solution(mesh):
    in_specs = (P(None, ("freq", "tile"), None, None), P(None, ("freq", "tile"), None), P())
    out_specs = P(None, ("freq", "tile"), None, None, None)
    return jax.shard_map(shards, mesh=mesh, in_specs=in_specs, out_specs=out_specs, check_vma=False)
```

```python
import functools

import jax
import jax.numpy as jnp
from jax import lax
from jax.experimental import pallas as pl
from jax.experimental.pallas import tpu as pltpu
from jax.sharding import PartitionSpec as P

CHANNELS_PER_BIN = 4
NB = 8
LINES = 2
DEPTH = NB // LINES
HALF = NB // 2
UP = (2, 3, 4, 5, 6, 7)
DOWN = (4, 5, 6, 7, 0, 1)
SHORT_UP = (0, 1)
SHORT_DOWN = (2, 3)
PARTS = 4
EXCHANGES = ((0, 1), (1, 4))
STEPS = ((0, 0), (0, 1), (1, 0), (0, 2), (1, 1), (2, 0), (1, 2), (3, 0), (2, 1), (3, 1), (2, 2), (3, 2))
GATHERS = {0: (0,), 2: (1,), 3: (2,), 4: (3,)}
TILES = {7: (0,), 9: (1,), 13: (2, 3)}
SIDE = 6
VMEM_BYTES = 56 * 1024 * 1024
STEP_BYTES = 4_000_000

KINDS = range(2 * NB)


def place(kind):
    return kind // 4, kind // 2 % 2, kind % 2


def along(name, kind):
    z, y, parity = place(kind)
    step = 1 if (name == "a") == (parity == 0) else -1
    if 0 <= z + step < DEPTH:
        return 4 * (z + step) + 2 * y + parity, True
    return 4 * z + 2 * y + 1 - parity, False


def upward(parity):
    return "a" if parity == 0 else "b"


def downward(parity):
    return "b" if parity == 0 else "a"


def my_kind(lanes):
    me = lax.axis_index("tile")
    return me // lanes * 2 + me % 2


def needed(u):
    return [(u - s) % NB for s in range(HALF + 1)]


def device_pairs(step, positions, lanes):
    pairs = []
    for g in range(positions):
        kind = step(g // lanes * 2 + g % 2)
        pairs.append((g, kind // 2 * lanes + g % lanes // 2 * 2 + kind % 2))
    return pairs


class Plan:
    def __init__(self):
        self.held = {}

    def own(self, name, part, blocks):
        self.held[name] = [[(part,) + place(k)[:2] + (b,) for b in blocks(place(k)[2])] for k in KINDS]

    def move(self, source, target, step):
        got = [None] * len(KINDS)
        for kind in KINDS:
            goal, useful = step(kind)
            items = self.held[source][kind]
            got[goal] = list(items) if useful else [None] * len(items)
        self.held[target] = got

    def find(self, kind, item, names):
        for name in names:
            if item in self.held[name][kind]:
                return name, self.held[name][kind].index(item)
        return None


def runs(picks):
    out = []
    for dst, name, src in picks:
        if out and out[-1][1] == name and out[-1][0] + out[-1][3] == dst and out[-1][2] + out[-1][3] == src:
            out[-1][3] += 1
        else:
            out.append([dst, name, src, 1])
    return [tuple(r) for r in out]


def copies_kernel(names, after, plan, patched, outs, lanes, *refs):
    ins = dict(zip(names, refs[: len(names)]))
    targets = dict(zip(list(patched) + list(outs), refs[len(names) + 1 + after : -3]))
    through, sems = refs[-2:]
    me = my_kind(lanes)
    for kind, todo in plan.items():

        @pl.when(me == kind)
        def _(todo=todo):
            started, onward, at = [], [], 0
            for i, (target, dst, name, src, length) in enumerate(todo):
                goal = targets[target].at[pl.ds(dst, length)]
                if target in patched:
                    onward.append((i, through.at[pl.ds(at, length)], goal))
                    goal = through.at[pl.ds(at, length)]
                    at += length
                copy = pltpu.make_async_copy(ins[name].at[pl.ds(src, length)], goal, sems.at[0, i])
                copy.start()
                started.append(copy)
            for copy in started:
                copy.wait()
            started = [pltpu.make_async_copy(src, goal, sems.at[1, i]) for i, src, goal in onward]
            for copy in started:
                copy.start()
            for copy in started:
                copy.wait()


def run_copies(arrays, names, after, plan, patched, outs, lanes):
    shape = arrays["a0.0"].shape[1:]
    dtype = arrays["a0.0"].dtype
    any_spec = pl.BlockSpec(memory_space=pl.ANY)
    out_shape = [jax.ShapeDtypeStruct(arrays[n].shape, dtype) for n in patched]
    out_shape += [jax.ShapeDtypeStruct((slots,) + shape, dtype) for slots in outs.values()]
    most = max(1, max(len(todo) for todo in plan.values()))
    token = arrays["token"]
    aliases = {names.index(n): i for i, n in enumerate(patched)}
    aliases[len(names)] = len(out_shape)
    got = pl.pallas_call(
        functools.partial(copies_kernel, names, len(after), plan, patched, list(outs), lanes),
        out_shape=out_shape + [jax.ShapeDtypeStruct(token.shape, token.dtype)],
        in_specs=[any_spec] * (len(names) + 1 + len(after)),
        out_specs=[any_spec] * len(patched) + [pl.BlockSpec(memory_space=pltpu.VMEM)] * len(outs) + [any_spec],
        scratch_shapes=[pltpu.VMEM((4,) + shape, dtype), pltpu.SemaphoreType.DMA((2, most))],
        input_output_aliases=aliases,
        compiler_params=pltpu.CompilerParams(vmem_limit_bytes=VMEM_BYTES),
        cost_estimate=pl.CostEstimate(flops=0, bytes_accessed=STEP_BYTES, transcendentals=0),
        name="pick",
    )(*[arrays[n] for n in names], token, *[arrays[n] for n in after])
    for n, value in zip(list(patched) + list(outs) + ["token"], got):
        arrays[n] = value


def gather_kernel(plan, lanes, start, own, token, a, b, token_out, sems):
    senders, rows = own.shape[0], own.shape[4]
    targets = {"a": a, "b": b}
    me = my_kind(lanes)
    for kind, todo in plan.items():

        @pl.when(me == kind)
        def _(todo=todo):
            started = []
            for lane in range(senders):
                at = pl.ds(lane * rows, rows)
                for i, (target, dst, src, length) in enumerate(todo):
                    copy = pltpu.make_async_copy(
                        own.at[lane, pl.ds(src, length), :, :, :, pl.ds(start, a.shape[-1])],
                        targets[target].at[pl.ds(dst, length), :, :, at],
                        sems.at[lane, i],
                    )
                    copy.start()
                    started.append(copy)
            for copy in started:
                copy.wait()


def run_gather(arrays, part, own, start, samples, plan, lanes):
    senders, _, two, split, rows, _ = own.shape
    shape = (two, split, senders * rows, samples)
    token = arrays["token"]
    any_spec = pl.BlockSpec(memory_space=pl.ANY)
    vmem_spec = pl.BlockSpec(memory_space=pltpu.VMEM)
    most = max(len(todo) for todo in plan.values())
    arrays["a0.%d" % part], arrays["b0.%d" % part], arrays["token"] = pl.pallas_call(
        functools.partial(gather_kernel, plan, lanes, start),
        out_shape=[jax.ShapeDtypeStruct((n,) + shape, own.dtype) for n in (len(UP), len(DOWN))]
        + [jax.ShapeDtypeStruct(token.shape, token.dtype)],
        in_specs=[any_spec] * 2,
        out_specs=[vmem_spec] * 2 + [any_spec],
        scratch_shapes=[pltpu.SemaphoreType.DMA((senders, most))],
        input_output_aliases={1: 2},
        compiler_params=pltpu.CompilerParams(vmem_limit_bytes=VMEM_BYTES),
        cost_estimate=pl.CostEstimate(flops=0, bytes_accessed=0, transcendentals=0),
        name="gather",
    )(own, token)


def tiles_kernel(names, plan, lanes, scale, first, last, *refs):
    ins = dict(zip(names, refs[: len(names)]))
    refs = refs[len(names) :]
    flag = acc = None
    if last:
        flag, refs = refs[0], refs[1:]
    if not first:
        acc, refs = refs[0], refs[1:]
    _, out, _, held, sems = refs
    me = my_kind(lanes)
    s = pl.program_id(0)

    @pl.when(s == 0)
    def _():
        for kind, todo in plan.items():

            @pl.when(me == kind)
            def _(todo=todo):
                for slot, row, name, src in todo:
                    pltpu.make_async_copy(ins[name].at[src], held.at[slot, :, :, row], sems.at[slot, row]).start()

    for row in range(NB):
        pltpu.make_async_copy(held.at[s, :, :, row], held.at[s, :, :, row], sems.at[s, row]).wait()
    rows = held.shape[2] * held.shape[3] * held.shape[4]
    samples = held.shape[5]

    def mul(a, b):
        return lax.dot_general(a, b, (((1,), (1,)), ((), ())), preferred_element_type=jnp.float32)

    ar = held[s, 0].reshape(rows, samples)
    ai = held[s, 1].reshape(rows, samples)
    br = held[0, 0].reshape(rows, samples)
    bi = held[0, 1].reshape(rows, samples)
    real = (mul(ar, br) + mul(ai, bi)) * scale
    imag = (mul(ar, bi) - mul(ai, br)) * scale
    if not first:
        real = real + acc[0, :, :rows]
        imag = imag + acc[0, :, rows:]
    if last:
        keep = jnp.logical_or(s < HALF, flag[0] == 1)
        real = jnp.where(keep, real, 0.0)
        imag = jnp.where(keep, imag, 0.0)
    out[0, :, :rows] = real
    out[0, :, rows:] = imag


def run_tiles(arrays, names, plan, lanes, scale, acc, flag):
    token = arrays["token"]
    shape = arrays[names[0]].shape[1:]
    rows = shape[1] * shape[2] * NB
    samples = shape[3]
    any_spec = pl.BlockSpec(memory_space=pl.ANY)
    tile_spec = pl.BlockSpec((1, rows, 2 * rows), lambda s: (s, 0, 0))
    operands = [arrays[n] for n in names]
    in_specs = [any_spec] * len(names)
    aliases = {}
    if flag is not None:
        operands.append(flag)
        in_specs.append(pl.BlockSpec(memory_space=pltpu.SMEM))
    if acc is not None:
        aliases = {len(operands): 0}
        operands.append(acc)
        in_specs.append(tile_spec)
    aliases[len(operands)] = 1
    operands.append(token)
    in_specs.append(any_spec)
    held = (HALF + 1, 2, shape[1], NB, shape[2], samples)
    result, arrays["token"] = pl.pallas_call(
        functools.partial(tiles_kernel, names, plan, lanes, scale, acc is None, flag is not None),
        grid=(HALF + 1,),
        out_shape=[
            jax.ShapeDtypeStruct((HALF + 1, rows, 2 * rows), jnp.float32),
            jax.ShapeDtypeStruct(token.shape, token.dtype),
        ],
        in_specs=in_specs,
        out_specs=[tile_spec, any_spec],
        scratch_shapes=[pltpu.VMEM(held, jnp.bfloat16), pltpu.SemaphoreType.DMA((HALF + 1, NB))],
        input_output_aliases=aliases,
        compiler_params=pltpu.CompilerParams(vmem_limit_bytes=VMEM_BYTES),
        cost_estimate=pl.CostEstimate(flops=0, bytes_accessed=0, transcendentals=0),
        name="tiles",
    )(*operands)
    return result


def exchange(voltages, scales, freq_count, lanes):
    samples = voltages.shape[3]
    rows = voltages.shape[1] // NB
    groups = scales.shape[2]
    split = (freq_count, lanes, rows, NB)
    factor = scales.astype(jnp.bfloat16).reshape(split + (1, groups, 1))
    x = voltages.reshape(split + (2, groups, samples // groups)) * factor
    x = x.reshape(split + (2, samples)).transpose(1, 3, 4, 0, 2, 5)
    if freq_count > 1:
        x = lax.all_to_all(x, "freq", 3, 3, tiled=True)
    positions = lax.axis_size("tile")
    groups = [list(range(g, g + lanes)) for g in range(0, positions, lanes)]
    x = lax.all_to_all(x, "tile", 0, 0, axis_index_groups=groups, tiled=True)
    if freq_count > 1:
        x = x.transpose(1, 2, 3, 0, 4, 5)
        x = x.reshape((1,) + x.shape[:3] + (lanes * rows, samples))
    return x


class Turn:
    def __init__(self, owns, lanes):
        self.owns, self.lanes = owns, lanes
        self.positions = lax.axis_size("tile")
        self.plan = Plan()
        self.arrays = {"token": jnp.zeros((8, 128), jnp.int32)}
        for part in range(len(owns)):
            self.plan.own("blocks.%d" % part, part, lambda parity: range(NB))
            self.plan.own("a0.%d" % part, part, lambda parity: DOWN if parity else UP)
            self.plan.own("b0.%d" % part, part, lambda parity: UP if parity else DOWN)
        self.sent = [set() for _ in KINDS]
        self.here = []
        self.crossed = []

    def move(self, source, target, step):
        self.plan.move(source, target, step)
        pairs = device_pairs(lambda kind: step(kind)[0], self.positions, self.lanes)
        self.arrays[target] = lax.ppermute(self.arrays[source], "tile", pairs)

    def gather(self, part):
        todo = {}
        for kind in KINDS:
            todo[kind] = []
            for name in "ab":
                blocks = [item[3] for item in self.plan.held["%s0.%d" % (name, part)][kind]]
                for d, _, src, length in runs([(i, "", b) for i, b in enumerate(blocks)]):
                    todo[kind].append((name, d, src, length))
        run_gather(self.arrays, part, *self.owns[part], todo, self.lanes)
        self.here += ["a0.%d" % part, "b0.%d" % part]

    def along(self, part, stage):
        for name in "ab":
            self.move("%s%d.%d" % (name, stage, part), "%s%d.%d" % (name, stage + 1, part), functools.partial(along, name))

    def arrived(self, part, stage):
        names = ["%s%d.%d" % (name, stage, part) for name in "ab"]
        self.here += names
        return names

    def choose(self, kind, most, parts):
        wanted = []
        y = place(kind)[1]
        for part in parts:
            for source in range(DEPTH):
                for b in needed(kind // 2 ^ 1):
                    item = (part, source, y, b)
                    where = self.plan.find(kind, item, self.here)
                    if item not in self.sent[kind] and where and len(wanted) < most:
                        wanted.append((item, where))
        wanted.sort(key=lambda w: w[1])
        self.sent[kind].update(w[0] for w in wanted)
        return wanted

    def prepare(self, part=None, stage=None, side=None, after=(), parts=None):
        todo = {kind: [] for kind in KINDS}
        patched, outs = [], {}
        if part is not None:
            patched = ["%s%d.%d" % (name, stage, part) for name in "ab"]
        if stage:
            for kind in KINDS:
                z, y, parity = place(kind)
                for low, way, blocks in ((z, upward, SHORT_UP), (DEPTH - 1 - z, downward, SHORT_DOWN)):
                    if low == stage - 1:
                        target, dst = "%s%d.%d" % (way(parity), stage, part), 2 * (stage - 1)
                        items = [(part, z, y, b) for b in blocks]
                        found = [self.plan.find(kind, item, ["a0.%d" % part, "b0.%d" % part]) for item in items]
                        for d, name, src, length in runs([(dst + i, n, k) for i, (n, k) in enumerate(found)]):
                            todo[kind].append((target, d, name, src, length))
                        self.plan.held[target][kind][dst : dst + len(items)] = items
        if side is not None:
            name, most = side
            chosen = [self.choose(kind, most, range(len(self.owns)) if parts is None else parts) for kind in KINDS]
            slots = max(len(c) for c in chosen)
            outs = {"side" + name: slots}
            for kind in KINDS:
                self.plan.held.setdefault("side" + name, []).append(
                    [w[0] for w in chosen[kind]] + [None] * (slots - len(chosen[kind]))
                )
                picks = [(i, n, k) for i, (_, (n, k)) in enumerate(chosen[kind])]
                todo[kind] += [("side" + name,) + r for r in runs(picks)]
        used = {t[2] for kind in KINDS for t in todo[kind]}
        names = [n for n in self.here if n in used or n in patched]
        after = [n for n in after if n not in names]
        run_copies(self.arrays, names, after, todo, patched, outs, self.lanes)
        if side is not None:
            self.move("side" + name, "got" + name, lambda kind: (kind ^ 2, True))
            self.crossed.append("got" + name)

    def tiles(self, part, scale, result, flag):
        names = [n for n in self.here if n.endswith(".%d" % part)] + self.crossed
        todo = {}
        for kind in KINDS:
            todo[kind] = []
            for s, b in enumerate(needed(kind // 2)):
                for row in range(NB):
                    where = self.plan.find(kind, (part, row // 2, row % 2, b), names)
                    assert where is not None
                    todo[kind].append((s, row) + where)
        used = {t[2] for kind in KINDS for t in todo[kind]}
        return run_tiles(self.arrays, [n for n in names if n in used], todo, self.lanes, scale, result, flag)


def shards(voltages, scales, owner_half):
    time_len = voltages.shape[3]
    group_len = time_len // scales.shape[2]
    freq_count = lax.axis_size("freq")
    lanes = CHANNELS_PER_BIN
    tile_pos = lax.axis_index("tile")
    chan_idx = lax.axis_index("freq") * lanes + tile_pos % lanes
    flag = lax.dynamic_slice(owner_half, (chan_idx, tile_pos // lanes), (1, 1)).reshape(1)
    samples = time_len // PARTS
    owns = []
    for first, last in EXCHANGES:
        start, stop = first * samples, last * samples
        own = exchange(
            voltages[..., start:stop], scales[..., start // group_len : stop // group_len], freq_count, lanes
        )
        owns += [(own, (part - first) * samples, samples) for part in range(first, last)]
    scale = 1.0 / time_len
    turn = Turn(owns, lanes)
    result = None
    known = 0
    for n, (part, stage) in enumerate(STEPS):
        for fresh in GATHERS.get(n, ()):
            turn.gather(fresh)
        done = []
        while known < n and (known <= n - 2 or STEPS[known][0] == part):
            done += turn.arrived(STEPS[known][0], STEPS[known][1] + 1)
            known += 1
        if n >= 1:
            done = done + ["got%d" % max(n - 2, 0)]
        turn.prepare(part, stage, side=(str(n), SIDE), after=done)
        turn.along(part, stage)
        for ready in TILES.get(n, ()):
            result = turn.tiles(ready, scale, result, None)
    for n in (len(STEPS), len(STEPS) + 1):
        done = ["got%d" % (n - 2)]
        while known < n - 1:
            done += turn.arrived(STEPS[known][0], STEPS[known][1] + 1)
            known += 1
        turn.prepare(side=(str(n), SIDE if n == len(STEPS) else 99), after=done)
    for ready in TILES.get(n, ()):
        result = turn.tiles(ready, scale, result, flag if ready == PARTS - 1 else None)
    return result[None, None]


def solution(mesh):
    in_specs = (P(None, ("freq", "tile"), None, None), P(None, ("freq", "tile"), None), P())
    out_specs = P(None, ("freq", "tile"), None, None, None)
    return jax.shard_map(shards, mesh=mesh, in_specs=in_specs, out_specs=out_specs, check_vma=False)
```

```python
import functools

import jax
import jax.numpy as jnp
from jax import lax
from jax.experimental import pallas as pl
from jax.experimental.pallas import tpu as pltpu
from jax.sharding import PartitionSpec as P

CHANNELS_PER_BIN = 4
NB = 8
LINES = 2
DEPTH = NB // LINES
HALF = NB // 2
UP = (2, 3, 4, 5, 6, 7)
DOWN = (4, 5, 6, 7, 0, 1)
SHORT_UP = (0, 1)
SHORT_DOWN = (2, 3)
PARTS = 4
EXCHANGES = ((0, 1), (1, 4))
STEPS = ((0, 0), (0, 1), (1, 0), (0, 2), (1, 1), (2, 0), (1, 2), (3, 0), (2, 1), (3, 1), (2, 2), (3, 2))
GATHERS = {0: (0,), 2: (1,), 3: (2,), 4: (3,)}
TILES = {7: (0,), 9: (1,), 13: (2, 3)}
SIDE = 6
VMEM_BYTES = 56 * 1024 * 1024
STEP_BYTES = 4_000_000

KINDS = range(2 * NB)


def place(kind):
    return kind // 4, kind // 2 % 2, kind % 2


def along(name, kind):
    z, y, parity = place(kind)
    step = 1 if (name == "a") == (parity == 0) else -1
    if 0 <= z + step < DEPTH:
        return 4 * (z + step) + 2 * y + parity, True
    return 4 * z + 2 * y + 1 - parity, False


def upward(parity):
    return "a" if parity == 0 else "b"


def downward(parity):
    return "b" if parity == 0 else "a"


def my_kind(lanes):
    me = lax.axis_index("tile")
    return me // lanes * 2 + me % 2


def needed(u):
    return [(u - s) % NB for s in range(HALF + 1)]


def device_pairs(step, positions, lanes):
    pairs = []
    for g in range(positions):
        kind = step(g // lanes * 2 + g % 2)
        pairs.append((g, kind // 2 * lanes + g % lanes // 2 * 2 + kind % 2))
    return pairs


class Plan:
    def __init__(self):
        self.held = {}

    def own(self, name, part, blocks):
        self.held[name] = [[(part,) + place(k)[:2] + (b,) for b in blocks(place(k)[2])] for k in KINDS]

    def move(self, source, target, step):
        got = [None] * len(KINDS)
        for kind in KINDS:
            goal, useful = step(kind)
            items = self.held[source][kind]
            got[goal] = list(items) if useful else [None] * len(items)
        self.held[target] = got

    def find(self, kind, item, names):
        for name in names:
            if item in self.held[name][kind]:
                return name, self.held[name][kind].index(item)
        return None


def runs(picks):
    out = []
    for dst, name, src in picks:
        if out and out[-1][1] == name and out[-1][0] + out[-1][3] == dst and out[-1][2] + out[-1][3] == src:
            out[-1][3] += 1
        else:
            out.append([dst, name, src, 1])
    return [tuple(r) for r in out]


def copies_kernel(names, after, plan, patched, outs, lanes, *refs):
    ins = dict(zip(names, refs[: len(names)]))
    targets = dict(zip(list(patched) + list(outs), refs[len(names) + 1 + after : -3]))
    through, sems = refs[-2:]
    me = my_kind(lanes)
    for kind, todo in plan.items():

        @pl.when(me == kind)
        def _(todo=todo):
            started, onward, at = [], [], 0
            for i, (target, dst, name, src, length) in enumerate(todo):
                goal = targets[target].at[pl.ds(dst, length)]
                if target in patched:
                    onward.append((i, through.at[pl.ds(at, length)], goal))
                    goal = through.at[pl.ds(at, length)]
                    at += length
                copy = pltpu.make_async_copy(ins[name].at[pl.ds(src, length)], goal, sems.at[0, i])
                copy.start()
                started.append(copy)
            for copy in started:
                copy.wait()
            started = [pltpu.make_async_copy(src, goal, sems.at[1, i]) for i, src, goal in onward]
            for copy in started:
                copy.start()
            for copy in started:
                copy.wait()


def run_copies(arrays, names, after, plan, patched, outs, lanes):
    shape = arrays["a0.0"].shape[1:]
    dtype = arrays["a0.0"].dtype
    any_spec = pl.BlockSpec(memory_space=pl.ANY)
    out_shape = [jax.ShapeDtypeStruct(arrays[n].shape, dtype) for n in patched]
    out_shape += [jax.ShapeDtypeStruct((slots,) + shape, dtype) for slots in outs.values()]
    most = max(1, max(len(todo) for todo in plan.values()))
    token = arrays["token"]
    aliases = {names.index(n): i for i, n in enumerate(patched)}
    aliases[len(names)] = len(out_shape)
    got = pl.pallas_call(
        functools.partial(copies_kernel, names, len(after), plan, patched, list(outs), lanes),
        out_shape=out_shape + [jax.ShapeDtypeStruct(token.shape, token.dtype)],
        in_specs=[any_spec] * (len(names) + 1 + len(after)),
        out_specs=[any_spec] * len(patched) + [pl.BlockSpec(memory_space=pltpu.VMEM)] * len(outs) + [any_spec],
        scratch_shapes=[pltpu.VMEM((4,) + shape, dtype), pltpu.SemaphoreType.DMA((2, most))],
        input_output_aliases=aliases,
        compiler_params=pltpu.CompilerParams(vmem_limit_bytes=VMEM_BYTES),
        cost_estimate=pl.CostEstimate(flops=0, bytes_accessed=STEP_BYTES, transcendentals=0),
        name="pick",
    )(*[arrays[n] for n in names], token, *[arrays[n] for n in after])
    for n, value in zip(list(patched) + list(outs) + ["token"], got):
        arrays[n] = value


def gather_kernel(plan, lanes, start, named, own, *refs):
    senders, rows = own.shape[0], own.shape[4]
    sems = refs[-1]
    targets = dict(zip(named, refs[-2 - len(named) : -2]))
    samples = targets[named[0]].shape[-1]
    me = my_kind(lanes)
    for kind, todo in plan.items():

        @pl.when(me == kind)
        def _(todo=todo):
            started = []
            for lane in range(senders):
                at = pl.ds(lane * rows, rows)
                for i, (target, dst, src, length) in enumerate(todo):
                    copy = pltpu.make_async_copy(
                        own.at[lane, pl.ds(src, length), :, :, :, pl.ds(start, samples)],
                        targets[target].at[pl.ds(dst, length), :, :, at],
                        sems.at[lane, i],
                    )
                    copy.start()
                    started.append(copy)
            for copy in started:
                copy.wait()


def run_gather(arrays, own, start, samples, plan, outs, lanes):
    senders, _, two, split, rows, _ = own.shape
    shape = (two, split, senders * rows, samples)
    any_spec = pl.BlockSpec(memory_space=pl.ANY)
    tokens = [arrays["token"]] if "token" in arrays else []
    most = max(len(todo) for todo in plan.values())
    got = pl.pallas_call(
        functools.partial(gather_kernel, plan, lanes, start, list(outs)),
        out_shape=[jax.ShapeDtypeStruct((n,) + shape, own.dtype) for n in outs.values()]
        + [jax.ShapeDtypeStruct((8, 128), jnp.int32)],
        in_specs=[any_spec] * (1 + len(tokens)),
        out_specs=[pl.BlockSpec(memory_space=pltpu.VMEM)] * len(outs) + [any_spec],
        scratch_shapes=[pltpu.SemaphoreType.DMA((senders, most))],
        input_output_aliases={1: len(outs)} if tokens else {},
        compiler_params=pltpu.CompilerParams(vmem_limit_bytes=VMEM_BYTES),
        cost_estimate=pl.CostEstimate(flops=0, bytes_accessed=0, transcendentals=0),
        name="gather",
    )(own, *tokens)
    for name, value in zip(list(outs) + ["token"], got):
        arrays[name] = value


def tiles_kernel(names, plan, lanes, scale, first, last, *refs):
    ins = dict(zip(names, refs[: len(names)]))
    refs = list(refs[len(names) :])
    flag = refs.pop(0) if last else None
    acc = None if first else refs.pop(0)
    _, out, _, held, sums, sems, in_sems, out_sems = refs
    me = my_kind(lanes)
    tiles = held.shape[0]
    for kind, todo in plan.items():

        @pl.when(me == kind)
        def _(todo=todo):
            for slot, row, name, src in todo:
                pltpu.make_async_copy(ins[name].at[src], held.at[slot, :, :, row], sems.at[slot, row]).start()

    if not first:
        for s in range(tiles):
            pltpu.make_async_copy(acc.at[s], sums.at[s], in_sems.at[s]).start()
    rows = held.shape[2] * held.shape[3] * held.shape[4]
    samples = held.shape[5]

    def mul(a, b):
        return lax.dot_general(a, b, (((1,), (1,)), ((), ())), preferred_element_type=jnp.float32)

    @pl.loop(0, tiles)
    def _(s):
        for row in range(NB):
            pltpu.make_async_copy(held.at[s, :, :, row], held.at[s, :, :, row], sems.at[s, row]).wait()
        if not first:
            pltpu.make_async_copy(acc.at[s], sums.at[s], in_sems.at[s]).wait()
        ar = held[s, 0].reshape(rows, samples)
        ai = held[s, 1].reshape(rows, samples)
        br = held[0, 0].reshape(rows, samples)
        bi = held[0, 1].reshape(rows, samples)
        real = (mul(ar, br) + mul(ai, bi)) * scale
        imag = (mul(ar, bi) - mul(ai, br)) * scale
        if not first:
            real = real + sums[s, :, :rows]
            imag = imag + sums[s, :, rows:]
        if last:
            keep = jnp.logical_or(s < tiles - 1, flag[0] == 1)
            real = jnp.where(keep, real, 0.0)
            imag = jnp.where(keep, imag, 0.0)
        sums[s, :, :rows] = real
        sums[s, :, rows:] = imag
        pltpu.make_async_copy(sums.at[s], out.at[s], out_sems.at[s]).start()

    for s in range(tiles):
        pltpu.make_async_copy(sums.at[s], out.at[s], out_sems.at[s]).wait()


def run_tiles(arrays, names, plan, lanes, scale, acc, flag):
    token = arrays["token"]
    shape = arrays[names[0]].shape[1:]
    rows = shape[1] * shape[2] * NB
    samples = shape[3]
    tiles = HALF + 1
    any_spec = pl.BlockSpec(memory_space=pl.ANY)
    operands = [arrays[n] for n in names]
    in_specs = [any_spec] * len(names)
    aliases = {}
    if flag is not None:
        operands.append(flag)
        in_specs.append(pl.BlockSpec(memory_space=pltpu.SMEM))
    if acc is not None:
        aliases = {len(operands): 0}
        operands.append(acc)
        in_specs.append(any_spec)
    aliases[len(operands)] = 1
    operands.append(token)
    in_specs.append(any_spec)
    result, arrays["token"] = pl.pallas_call(
        functools.partial(tiles_kernel, names, plan, lanes, scale, acc is None, flag is not None),
        out_shape=[
            jax.ShapeDtypeStruct((tiles, rows, 2 * rows), jnp.float32),
            jax.ShapeDtypeStruct(token.shape, token.dtype),
        ],
        in_specs=in_specs,
        out_specs=[any_spec, any_spec],
        scratch_shapes=[
            pltpu.VMEM((tiles, 2, shape[1], NB, shape[2], samples), jnp.bfloat16),
            pltpu.VMEM((tiles, rows, 2 * rows), jnp.float32),
            pltpu.SemaphoreType.DMA((tiles, NB)),
            pltpu.SemaphoreType.DMA((tiles,)),
            pltpu.SemaphoreType.DMA((tiles,)),
        ],
        input_output_aliases=aliases,
        compiler_params=pltpu.CompilerParams(vmem_limit_bytes=VMEM_BYTES),
        cost_estimate=pl.CostEstimate(flops=0, bytes_accessed=0, transcendentals=0),
        name="tiles",
    )(*operands)
    return result


def exchange(voltages, scales, freq_count, lanes):
    samples = voltages.shape[3]
    rows = voltages.shape[1] // NB
    groups = scales.shape[2]
    split = (freq_count, lanes, rows, NB)
    factor = scales.astype(jnp.bfloat16).reshape(split + (1, groups, 1))
    x = voltages.reshape(split + (2, groups, samples // groups)) * factor
    x = x.reshape(split + (2, samples)).transpose(1, 3, 4, 0, 2, 5)
    if freq_count > 1:
        x = lax.all_to_all(x, "freq", 3, 3, tiled=True)
    positions = lax.axis_size("tile")
    groups = [list(range(g, g + lanes)) for g in range(0, positions, lanes)]
    x = lax.all_to_all(x, "tile", 0, 0, axis_index_groups=groups, tiled=True)
    if freq_count > 1:
        x = x.transpose(1, 2, 3, 0, 4, 5)
        x = x.reshape((1,) + x.shape[:3] + (lanes * rows, samples))
    return x


class Turn:
    def __init__(self, owns, lanes):
        self.owns, self.lanes = owns, lanes
        self.positions = lax.axis_size("tile")
        self.plan = Plan()
        self.arrays = {}
        for part in range(len(owns)):
            self.plan.own("blocks.%d" % part, part, lambda parity: range(NB))
            self.plan.own("a0.%d" % part, part, lambda parity: DOWN if parity else UP)
            self.plan.own("b0.%d" % part, part, lambda parity: UP if parity else DOWN)
        self.sent = [set() for _ in KINDS]
        self.here = []
        self.crossed = []

    def move(self, source, target, step):
        self.plan.move(source, target, step)
        pairs = device_pairs(lambda kind: step(kind)[0], self.positions, self.lanes)
        self.arrays[target] = lax.ppermute(self.arrays[source], "tile", pairs)

    def gather(self, part, side=None):
        todo, outs = {}, {"a0.%d" % part: len(UP), "b0.%d" % part: len(DOWN)}
        if side is not None:
            outs["side" + side] = HALF + 1
        for kind in KINDS:
            todo[kind] = []
            for name in ("a0.%d" % part, "b0.%d" % part):
                blocks = [item[3] for item in self.plan.held[name][kind]]
                for d, _, src, length in runs([(i, "", b) for i, b in enumerate(blocks)]):
                    todo[kind].append((name, d, src, length))
            if side is not None:
                items = [item for item, _ in self.choose(kind, HALF + 1, [part], ["blocks.%d" % part])]
                self.plan.held.setdefault("side" + side, []).append(items)
                for d, _, src, length in runs([(i, "", item[3]) for i, item in enumerate(items)]):
                    todo[kind].append(("side" + side, d, src, length))
        run_gather(self.arrays, *self.owns[part], todo, outs, self.lanes)
        self.here += ["a0.%d" % part, "b0.%d" % part]
        if side is not None:
            self.across(side)

    def across(self, name):
        self.move("side" + name, "got" + name, lambda kind: (kind ^ 2, True))
        self.crossed.append("got" + name)

    def along(self, part, stage):
        for name in "ab":
            self.move("%s%d.%d" % (name, stage, part), "%s%d.%d" % (name, stage + 1, part), functools.partial(along, name))

    def arrived(self, part, stage):
        names = ["%s%d.%d" % (name, stage, part) for name in "ab"]
        self.here += names
        return names

    def choose(self, kind, most, parts, names):
        wanted = []
        y = place(kind)[1]
        for part in parts:
            for source in range(DEPTH):
                for b in needed(kind // 2 ^ 1):
                    item = (part, source, y, b)
                    where = self.plan.find(kind, item, names)
                    if item not in self.sent[kind] and where and len(wanted) < most:
                        wanted.append((item, where))
        wanted.sort(key=lambda w: w[1])
        self.sent[kind].update(w[0] for w in wanted)
        return wanted

    def prepare(self, part=None, stage=None, side=None, after=()):
        todo = {kind: [] for kind in KINDS}
        patched, outs = [], {}
        if part is not None:
            patched = ["%s%d.%d" % (name, stage, part) for name in "ab"]
        if stage:
            for kind in KINDS:
                z, y, parity = place(kind)
                for low, way, blocks in ((z, upward, SHORT_UP), (DEPTH - 1 - z, downward, SHORT_DOWN)):
                    if low == stage - 1:
                        target, dst = "%s%d.%d" % (way(parity), stage, part), 2 * (stage - 1)
                        items = [(part, z, y, b) for b in blocks]
                        found = [self.plan.find(kind, item, ["a0.%d" % part, "b0.%d" % part]) for item in items]
                        for d, name, src, length in runs([(dst + i, n, k) for i, (n, k) in enumerate(found)]):
                            todo[kind].append((target, d, name, src, length))
                        self.plan.held[target][kind][dst : dst + len(items)] = items
        if side is not None:
            name, most = side
            chosen = [self.choose(kind, most, range(len(self.owns)), self.here) for kind in KINDS]
            slots = max(len(c) for c in chosen)
            outs = {"side" + name: slots}
            for kind in KINDS:
                self.plan.held.setdefault("side" + name, []).append(
                    [w[0] for w in chosen[kind]] + [None] * (slots - len(chosen[kind]))
                )
                picks = [(i, n, k) for i, (_, (n, k)) in enumerate(chosen[kind])]
                todo[kind] += [("side" + name,) + r for r in runs(picks)]
        used = {t[2] for kind in KINDS for t in todo[kind]}
        names = [n for n in self.here if n in used or n in patched]
        after = [n for n in after if n not in names]
        run_copies(self.arrays, names, after, todo, patched, outs, self.lanes)
        if side is not None:
            self.across(name)

    def tiles(self, part, scale, result, flag):
        names = [n for n in self.here if n.endswith(".%d" % part)] + self.crossed
        todo = {}
        for kind in KINDS:
            todo[kind] = []
            for s, b in enumerate(needed(kind // 2)):
                for row in range(NB):
                    where = self.plan.find(kind, (part, row // 2, row % 2, b), names)
                    assert where is not None
                    todo[kind].append((s, row) + where)
        used = {t[2] for kind in KINDS for t in todo[kind]}
        return run_tiles(self.arrays, [n for n in names if n in used], todo, self.lanes, scale, result, flag)


def shards(voltages, scales, owner_half):
    time_len = voltages.shape[3]
    group_len = time_len // scales.shape[2]
    freq_count = lax.axis_size("freq")
    lanes = CHANNELS_PER_BIN
    tile_pos = lax.axis_index("tile")
    chan_idx = lax.axis_index("freq") * lanes + tile_pos % lanes
    flag = lax.dynamic_slice(owner_half, (chan_idx, tile_pos // lanes), (1, 1)).reshape(1)
    samples = time_len // PARTS
    owns = []
    for first, last in EXCHANGES:
        start, stop = first * samples, last * samples
        own = exchange(
            voltages[..., start:stop], scales[..., start // group_len : stop // group_len], freq_count, lanes
        )
        owns += [(own, (part - first) * samples, samples) for part in range(first, last)]
    scale = 1.0 / time_len
    turn = Turn(owns, lanes)
    result = None
    known = 0
    for n, (part, stage) in enumerate(STEPS):
        for fresh in GATHERS.get(n, ()):
            turn.gather(fresh, "0" if n == 0 else None)
        done = []
        while known < n and (known <= n - 2 or STEPS[known][0] == part):
            done += turn.arrived(STEPS[known][0], STEPS[known][1] + 1)
            known += 1
        if n >= 1:
            done = done + ["got%d" % max(n - 2, 0)]
        if n >= 1:
            turn.prepare(part, stage, side=(str(n), SIDE), after=done)
        turn.along(part, stage)
        for ready in TILES.get(n, ()):
            result = turn.tiles(ready, scale, result, None)
    for n in (len(STEPS), len(STEPS) + 1):
        done = ["got%d" % (n - 2)]
        while known < n - 1:
            done += turn.arrived(STEPS[known][0], STEPS[known][1] + 1)
            known += 1
        turn.prepare(side=(str(n), SIDE if n == len(STEPS) else 99), after=done)
    for ready in TILES.get(n, ()):
        result = turn.tiles(ready, scale, result, flag if ready == PARTS - 1 else None)
    return result[None, None]


def solution(mesh):
    in_specs = (P(None, ("freq", "tile"), None, None), P(None, ("freq", "tile"), None), P())
    out_specs = P(None, ("freq", "tile"), None, None, None)
    return jax.shard_map(shards, mesh=mesh, in_specs=in_specs, out_specs=out_specs, check_vma=False)
```

```python
import functools

import jax
import jax.numpy as jnp
from jax import lax
from jax.experimental import pallas as pl
from jax.experimental.pallas import tpu as pltpu
from jax.sharding import PartitionSpec as P

CHANNELS_PER_BIN = 4
NB = 8
LINES = 2
DEPTH = NB // LINES
HALF = NB // 2
UP = (2, 3, 4, 5, 6, 7)
DOWN = (4, 5, 6, 7, 0, 1)
SHORT_UP = (0, 1)
SHORT_DOWN = (2, 3)
PARTS = 4
EXCHANGES = ((0, 1), (1, 4))
STEPS = ((0, 0), (0, 1), (1, 0), (0, 2), (1, 1), (2, 0), (1, 2), (3, 0), (2, 1), (3, 1), (2, 2), (3, 2))
GATHERS = {0: (0,), 2: (1,), 3: (2,), 4: (3,)}
TILES = {7: (0,), 9: (1,), 13: (2, 3)}
SIDE = 6
VMEM_BYTES = 62 * 1024 * 1024
STEP_BYTES = 4_000_000

KINDS = range(2 * NB)


def place(kind):
    return kind // 4, kind // 2 % 2, kind % 2


def along(name, kind):
    z, y, parity = place(kind)
    step = 1 if (name == "a") == (parity == 0) else -1
    if 0 <= z + step < DEPTH:
        return 4 * (z + step) + 2 * y + parity, True
    return 4 * z + 2 * y + 1 - parity, False


def upward(parity):
    return "a" if parity == 0 else "b"


def downward(parity):
    return "b" if parity == 0 else "a"


def my_kind(lanes):
    me = lax.axis_index("tile")
    return me // lanes * 2 + me % 2


def needed(u):
    return [(u - s) % NB for s in range(HALF + 1)]


def device_pairs(step, positions, lanes):
    pairs = []
    for g in range(positions):
        kind = step(g // lanes * 2 + g % 2)
        pairs.append((g, kind // 2 * lanes + g % lanes // 2 * 2 + kind % 2))
    return pairs


class Plan:
    def __init__(self):
        self.held = {}

    def own(self, name, part, blocks):
        self.held[name] = [[(part,) + place(k)[:2] + (b,) for b in blocks(place(k)[2])] for k in KINDS]

    def move(self, source, target, step):
        got = [None] * len(KINDS)
        for kind in KINDS:
            goal, useful = step(kind)
            items = self.held[source][kind]
            got[goal] = list(items) if useful else [None] * len(items)
        self.held[target] = got

    def find(self, kind, item, names):
        for name in names:
            if item in self.held[name][kind]:
                return name, self.held[name][kind].index(item)
        return None


def runs(picks):
    out = []
    for dst, name, src in picks:
        if out and out[-1][1] == name and out[-1][0] + out[-1][3] == dst and out[-1][2] + out[-1][3] == src:
            out[-1][3] += 1
        else:
            out.append([dst, name, src, 1])
    return [tuple(r) for r in out]


def copies_kernel(names, after, plan, patched, outs, lanes, *refs):
    ins = dict(zip(names, refs[: len(names)]))
    targets = dict(zip(list(patched) + list(outs), refs[len(names) + 1 + after : -3]))
    through, sems = refs[-2:]
    me = my_kind(lanes)
    for kind, todo in plan.items():

        @pl.when(me == kind)
        def _(todo=todo):
            started, onward, at = [], [], 0
            for i, (target, dst, name, src, length) in enumerate(todo):
                goal = targets[target].at[pl.ds(dst, length)]
                if target in patched:
                    onward.append((i, through.at[pl.ds(at, length)], goal))
                    goal = through.at[pl.ds(at, length)]
                    at += length
                copy = pltpu.make_async_copy(ins[name].at[pl.ds(src, length)], goal, sems.at[0, i])
                copy.start()
                started.append(copy)
            for copy in started:
                copy.wait()
            started = [pltpu.make_async_copy(src, goal, sems.at[1, i]) for i, src, goal in onward]
            for copy in started:
                copy.start()
            for copy in started:
                copy.wait()


def run_copies(arrays, names, after, plan, patched, outs, lanes):
    shape = arrays["a0.0"].shape[1:]
    dtype = arrays["a0.0"].dtype
    any_spec = pl.BlockSpec(memory_space=pl.ANY)
    out_shape = [jax.ShapeDtypeStruct(arrays[n].shape, dtype) for n in patched]
    out_shape += [jax.ShapeDtypeStruct((slots,) + shape, dtype) for slots in outs.values()]
    most = max(1, max(len(todo) for todo in plan.values()))
    token = arrays["token"]
    aliases = {names.index(n): i for i, n in enumerate(patched)}
    aliases[len(names)] = len(out_shape)
    got = pl.pallas_call(
        functools.partial(copies_kernel, names, len(after), plan, patched, list(outs), lanes),
        out_shape=out_shape + [jax.ShapeDtypeStruct(token.shape, token.dtype)],
        in_specs=[any_spec] * (len(names) + 1 + len(after)),
        out_specs=[any_spec] * len(patched) + [pl.BlockSpec(memory_space=pltpu.VMEM)] * len(outs) + [any_spec],
        scratch_shapes=[pltpu.VMEM((4,) + shape, dtype), pltpu.SemaphoreType.DMA((2, most))],
        input_output_aliases=aliases,
        compiler_params=pltpu.CompilerParams(vmem_limit_bytes=VMEM_BYTES),
        cost_estimate=pl.CostEstimate(flops=0, bytes_accessed=STEP_BYTES, transcendentals=0),
        name="pick",
    )(*[arrays[n] for n in names], token, *[arrays[n] for n in after])
    for n, value in zip(list(patched) + list(outs) + ["token"], got):
        arrays[n] = value


def gather_kernel(plan, lanes, start, named, own, *refs):
    senders, rows = own.shape[0], own.shape[4]
    sems = refs[-1]
    targets = dict(zip(named, refs[-2 - len(named) : -2]))
    samples = targets[named[0]].shape[-1]
    me = my_kind(lanes)
    for kind, todo in plan.items():

        @pl.when(me == kind)
        def _(todo=todo):
            started = []
            for lane in range(senders):
                at = pl.ds(lane * rows, rows)
                for i, (target, dst, src, length) in enumerate(todo):
                    copy = pltpu.make_async_copy(
                        own.at[lane, pl.ds(src, length), :, :, :, pl.ds(start, samples)],
                        targets[target].at[pl.ds(dst, length), :, :, at],
                        sems.at[lane, i],
                    )
                    copy.start()
                    started.append(copy)
            for copy in started:
                copy.wait()


def run_gather(arrays, own, start, samples, plan, outs, lanes):
    senders, _, two, split, rows, _ = own.shape
    shape = (two, split, senders * rows, samples)
    any_spec = pl.BlockSpec(memory_space=pl.ANY)
    tokens = [arrays["token"]] if "token" in arrays else []
    most = max(len(todo) for todo in plan.values())
    got = pl.pallas_call(
        functools.partial(gather_kernel, plan, lanes, start, list(outs)),
        out_shape=[jax.ShapeDtypeStruct((n,) + shape, own.dtype) for n in outs.values()]
        + [jax.ShapeDtypeStruct((8, 128), jnp.int32)],
        in_specs=[any_spec] * (1 + len(tokens)),
        out_specs=[pl.BlockSpec(memory_space=pltpu.VMEM)] * len(outs) + [any_spec],
        scratch_shapes=[pltpu.SemaphoreType.DMA((senders, most))],
        input_output_aliases={1: len(outs)} if tokens else {},
        compiler_params=pltpu.CompilerParams(vmem_limit_bytes=VMEM_BYTES),
        cost_estimate=pl.CostEstimate(flops=0, bytes_accessed=0, transcendentals=0),
        name="gather",
    )(own, *tokens)
    for name, value in zip(list(outs) + ["token"], got):
        arrays[name] = value


def tiles_kernel(names, plan, lanes, scale, first, last, *refs):
    ins = dict(zip(names, refs[: len(names)]))
    refs = list(refs[len(names) :])
    flag = refs.pop(0) if last else None
    acc = None if first else refs.pop(0)
    _, out, _, held, sums, sems, in_sems, out_sems = refs
    me = my_kind(lanes)
    tiles = held.shape[0]
    for kind, todo in plan.items():

        @pl.when(me == kind)
        def _(todo=todo):
            for slot, row, name, src in todo:
                pltpu.make_async_copy(ins[name].at[src], held.at[slot, :, :, row], sems.at[slot, row]).start()

    if not first:
        for s in range(tiles):
            pltpu.make_async_copy(acc.at[s], sums.at[s], in_sems.at[s]).start()
    rows = held.shape[2] * held.shape[3] * held.shape[4]
    samples = held.shape[5]

    def mul(a, b):
        return lax.dot_general(a, b, (((1,), (1,)), ((), ())), preferred_element_type=jnp.float32)

    @pl.loop(0, tiles)
    def _(s):
        for row in range(NB):
            pltpu.make_async_copy(held.at[s, :, :, row], held.at[s, :, :, row], sems.at[s, row]).wait()
        if not first:
            pltpu.make_async_copy(acc.at[s], sums.at[s], in_sems.at[s]).wait()
        ar = held[s, 0].reshape(rows, samples)
        ai = held[s, 1].reshape(rows, samples)
        br = held[0, 0].reshape(rows, samples)
        bi = held[0, 1].reshape(rows, samples)
        real = (mul(ar, br) + mul(ai, bi)) * scale
        imag = (mul(ar, bi) - mul(ai, br)) * scale
        if not first:
            real = real + sums[s, :, :rows]
            imag = imag + sums[s, :, rows:]
        if last:
            keep = jnp.logical_or(s < tiles - 1, flag[0] == 1)
            real = jnp.where(keep, real, 0.0)
            imag = jnp.where(keep, imag, 0.0)
        sums[s, :, :rows] = real
        sums[s, :, rows:] = imag
        pltpu.make_async_copy(sums.at[s], out.at[s], out_sems.at[s]).start()

    for s in range(tiles):
        pltpu.make_async_copy(sums.at[s], out.at[s], out_sems.at[s]).wait()


def run_tiles(arrays, names, plan, lanes, scale, acc, flag):
    token = arrays["token"]
    shape = arrays[names[0]].shape[1:]
    rows = shape[1] * shape[2] * NB
    samples = shape[3]
    tiles = HALF + 1
    any_spec = pl.BlockSpec(memory_space=pl.ANY)
    operands = [arrays[n] for n in names]
    in_specs = [any_spec] * len(names)
    aliases = {}
    if flag is not None:
        operands.append(flag)
        in_specs.append(pl.BlockSpec(memory_space=pltpu.SMEM))
    if acc is not None:
        aliases = {len(operands): 0}
        operands.append(acc)
        in_specs.append(any_spec)
    aliases[len(operands)] = 1
    operands.append(token)
    in_specs.append(any_spec)
    result, arrays["token"] = pl.pallas_call(
        functools.partial(tiles_kernel, names, plan, lanes, scale, acc is None, flag is not None),
        out_shape=[
            jax.ShapeDtypeStruct((tiles, rows, 2 * rows), jnp.float32),
            jax.ShapeDtypeStruct(token.shape, token.dtype),
        ],
        in_specs=in_specs,
        out_specs=[any_spec, any_spec],
        scratch_shapes=[
            pltpu.VMEM((tiles, 2, shape[1], NB, shape[2], samples), jnp.bfloat16),
            pltpu.VMEM((tiles, rows, 2 * rows), jnp.float32),
            pltpu.SemaphoreType.DMA((tiles, NB)),
            pltpu.SemaphoreType.DMA((tiles,)),
            pltpu.SemaphoreType.DMA((tiles,)),
        ],
        input_output_aliases=aliases,
        compiler_params=pltpu.CompilerParams(vmem_limit_bytes=VMEM_BYTES),
        cost_estimate=pl.CostEstimate(flops=0, bytes_accessed=0, transcendentals=0),
        name="tiles",
    )(*operands)
    return result


def exchange(voltages, scales, freq_count, lanes):
    samples = voltages.shape[3]
    rows = voltages.shape[1] // NB
    groups = scales.shape[2]
    split = (freq_count, lanes, rows, NB)
    factor = scales.astype(jnp.bfloat16).reshape(split + (1, groups, 1))
    x = voltages.reshape(split + (2, groups, samples // groups)) * factor
    x = x.reshape(split + (2, samples)).transpose(1, 3, 4, 0, 2, 5)
    if freq_count > 1:
        x = lax.all_to_all(x, "freq", 3, 3, tiled=True)
    positions = lax.axis_size("tile")
    groups = [list(range(g, g + lanes)) for g in range(0, positions, lanes)]
    x = lax.all_to_all(x, "tile", 0, 0, axis_index_groups=groups, tiled=True)
    if freq_count > 1:
        x = x.transpose(1, 2, 3, 0, 4, 5)
        x = x.reshape((1,) + x.shape[:3] + (lanes * rows, samples))
    return x


class Turn:
    def __init__(self, owns, lanes):
        self.owns, self.lanes = owns, lanes
        self.positions = lax.axis_size("tile")
        self.plan = Plan()
        self.arrays = {}
        for part in range(len(owns)):
            self.plan.own("blocks.%d" % part, part, lambda parity: range(NB))
            self.plan.own("a0.%d" % part, part, lambda parity: DOWN if parity else UP)
            self.plan.own("b0.%d" % part, part, lambda parity: UP if parity else DOWN)
        self.sent = [set() for _ in KINDS]
        self.here = []
        self.crossed = []

    def move(self, source, target, step):
        self.plan.move(source, target, step)
        pairs = device_pairs(lambda kind: step(kind)[0], self.positions, self.lanes)
        self.arrays[target] = lax.ppermute(self.arrays[source], "tile", pairs)

    def gather(self, part, side=None):
        todo, outs = {}, {"a0.%d" % part: len(UP), "b0.%d" % part: len(DOWN)}
        if side is not None:
            outs["side" + side] = HALF + 1
        for kind in KINDS:
            todo[kind] = []
            for name in ("a0.%d" % part, "b0.%d" % part):
                blocks = [item[3] for item in self.plan.held[name][kind]]
                for d, _, src, length in runs([(i, "", b) for i, b in enumerate(blocks)]):
                    todo[kind].append((name, d, src, length))
            if side is not None:
                items = [item for item, _ in self.choose(kind, HALF + 1, [part], ["blocks.%d" % part])]
                self.plan.held.setdefault("side" + side, []).append(items)
                for d, _, src, length in runs([(i, "", item[3]) for i, item in enumerate(items)]):
                    todo[kind].append(("side" + side, d, src, length))
        run_gather(self.arrays, *self.owns[part], todo, outs, self.lanes)
        self.here += ["a0.%d" % part, "b0.%d" % part]
        if side is not None:
            self.across(side)

    def across(self, name):
        self.move("side" + name, "got" + name, lambda kind: (kind ^ 2, True))
        self.crossed.append("got" + name)

    def along(self, part, stage):
        for name in "ab":
            self.move("%s%d.%d" % (name, stage, part), "%s%d.%d" % (name, stage + 1, part), functools.partial(along, name))

    def arrived(self, part, stage):
        names = ["%s%d.%d" % (name, stage, part) for name in "ab"]
        self.here += names
        return names

    def choose(self, kind, most, parts, names):
        wanted = []
        y = place(kind)[1]
        for part in parts:
            for source in range(DEPTH):
                for b in needed(kind // 2 ^ 1):
                    item = (part, source, y, b)
                    where = self.plan.find(kind, item, names)
                    if item not in self.sent[kind] and where and len(wanted) < most:
                        wanted.append((item, where))
        wanted.sort(key=lambda w: w[1])
        self.sent[kind].update(w[0] for w in wanted)
        return wanted

    def prepare(self, part=None, stage=None, side=None, after=()):
        todo = {kind: [] for kind in KINDS}
        patched, outs = [], {}
        if part is not None:
            patched = ["%s%d.%d" % (name, stage, part) for name in "ab"]
        if stage:
            for kind in KINDS:
                z, y, parity = place(kind)
                for low, way, blocks in ((z, upward, SHORT_UP), (DEPTH - 1 - z, downward, SHORT_DOWN)):
                    if low == stage - 1:
                        target, dst = "%s%d.%d" % (way(parity), stage, part), 2 * (stage - 1)
                        items = [(part, z, y, b) for b in blocks]
                        found = [self.plan.find(kind, item, ["a0.%d" % part, "b0.%d" % part]) for item in items]
                        for d, name, src, length in runs([(dst + i, n, k) for i, (n, k) in enumerate(found)]):
                            todo[kind].append((target, d, name, src, length))
                        self.plan.held[target][kind][dst : dst + len(items)] = items
        if side is not None:
            name, most = side
            chosen = [self.choose(kind, most, range(len(self.owns)), self.here) for kind in KINDS]
            slots = max(len(c) for c in chosen)
            outs = {"side" + name: slots}
            for kind in KINDS:
                self.plan.held.setdefault("side" + name, []).append(
                    [w[0] for w in chosen[kind]] + [None] * (slots - len(chosen[kind]))
                )
                picks = [(i, n, k) for i, (_, (n, k)) in enumerate(chosen[kind])]
                todo[kind] += [("side" + name,) + r for r in runs(picks)]
        used = {t[2] for kind in KINDS for t in todo[kind]}
        names = [n for n in self.here if n in used or n in patched]
        after = [n for n in after if n not in names]
        run_copies(self.arrays, names, after, todo, patched, outs, self.lanes)
        if side is not None:
            self.across(name)

    def tiles(self, part, scale, result, flag):
        names = [n for n in self.here if n.endswith(".%d" % part)] + self.crossed
        todo = {}
        for kind in KINDS:
            todo[kind] = []
            for s, b in enumerate(needed(kind // 2)):
                for row in range(NB):
                    where = self.plan.find(kind, (part, row // 2, row % 2, b), names)
                    assert where is not None
                    todo[kind].append((s, row) + where)
        used = {t[2] for kind in KINDS for t in todo[kind]}
        return run_tiles(self.arrays, [n for n in names if n in used], todo, self.lanes, scale, result, flag)


def shards(voltages, scales, owner_half):
    time_len = voltages.shape[3]
    group_len = time_len // scales.shape[2]
    freq_count = lax.axis_size("freq")
    lanes = CHANNELS_PER_BIN
    tile_pos = lax.axis_index("tile")
    chan_idx = lax.axis_index("freq") * lanes + tile_pos % lanes
    flag = lax.dynamic_slice(owner_half, (chan_idx, tile_pos // lanes), (1, 1)).reshape(1)
    samples = time_len // PARTS
    owns = []
    for first, last in EXCHANGES:
        start, stop = first * samples, last * samples
        own = exchange(
            voltages[..., start:stop], scales[..., start // group_len : stop // group_len], freq_count, lanes
        )
        owns += [(own, (part - first) * samples, samples) for part in range(first, last)]
    scale = 1.0 / time_len
    turn = Turn(owns, lanes)
    result = None
    known = 0
    for n, (part, stage) in enumerate(STEPS):
        for fresh in GATHERS.get(n, ()):
            turn.gather(fresh, "0" if n == 0 else None)
        done = []
        while known < n and (known <= n - 2 or STEPS[known][0] == part):
            done += turn.arrived(STEPS[known][0], STEPS[known][1] + 1)
            known += 1
        if n >= 1:
            done = done + ["got%d" % max(n - 2, 0)]
        if n >= 1:
            turn.prepare(part, stage, side=(str(n), SIDE), after=done)
        turn.along(part, stage)
        for ready in TILES.get(n, ()):
            result = turn.tiles(ready, scale, result, None)
    for n in (len(STEPS), len(STEPS) + 1):
        done = ["got%d" % (n - 2)]
        while known < n - 1:
            done += turn.arrived(STEPS[known][0], STEPS[known][1] + 1)
            known += 1
        turn.prepare(side=(str(n), SIDE if n == len(STEPS) else 99), after=done)
    for ready in TILES.get(n, ()):
        result = turn.tiles(ready, scale, result, flag if ready == PARTS - 1 else None)
    return result[None, None]


def solution(mesh):
    in_specs = (P(None, ("freq", "tile"), None, None), P(None, ("freq", "tile"), None), P())
    out_specs = P(None, ("freq", "tile"), None, None, None)
    return jax.shard_map(shards, mesh=mesh, in_specs=in_specs, out_specs=out_specs, check_vma=False)
```
